32 devices in a mesh: rows: 8 (over y, x, core), cols: 4 (over z).
Axes of the slice: x: 2, y: 2, z: 4, core: 2. Of those that a mesh axis runs over, the one named last changes fastest.
Arguments:
- sheet: bfloat16 [8, 1024, 1024], P('cols', 'rows'), may hold values from -600 to 600
- w_in: bfloat16 [1024, 16, 384], P(None, 'cols'), may hold values from -0.1875 to 0.1875
- w_out: bfloat16 [16, 128, 1024], P('cols'), may hold values from -0.125 to 0.125
Outputs:
- mixed: bfloat16 [8, 1024, 1024], P('cols', 'rows')
The draws below stay inside these ranges and needn't reach their ends.
All inputs are finite; a program needn't handle non-finite values.
Results may differ from the reference program's by a relative error of at most 0.0067.
Values may be sent and summed in bfloat16 or wider, within the bound.
A program may use at most 128 MiB of HBM per device.

```python
import math
import jax
import jax.numpy as jnp
from jax import lax

D = 1024
HEADS = 16
HDIM = 64
ROW_DEV = 128
ROWS = 1024
COLS = 8


def draw_sheet(key, part):
    key_base, key_cell, key_feat = jax.random.split(jax.random.fold_in(key, 11), 3)
    base = jnp.clip(jax.random.normal(key_base, (COLS, ROWS, D), jnp.float32), -6.0, 6.0)
    cell_scale = jnp.exp(jax.random.uniform(key_cell, (COLS, ROWS, 1), jnp.float32, 0.0, math.log(10.0)))
    feat_scale = jnp.exp(jax.random.uniform(key_feat, (1, 1, D), jnp.float32, 0.0, math.log(10.0)))
    return (base * cell_scale * feat_scale).astype(jnp.bfloat16)


def level_of(stream_key, dims, cuts, smallest, largest):
    gain, own = 1.0, jax.random.fold_in(stream_key, 6)
    for axis_at, shards_of in cuts:
        steps = jnp.exp(jax.random.uniform(jax.random.fold_in(own, axis_at), (shards_of,), jnp.float32, smallest / len(cuts), largest / len(cuts)))
        gain = gain * jnp.repeat(steps, dims[axis_at] // shards_of).reshape([-1 if axis == axis_at else 1 for axis in range(len(dims))])
    return gain


def gaussian(stream_key, extent, deviation, bound, cuts=(), dtype=jnp.bfloat16):
    level = level_of(stream_key, extent, cuts, -0.22, 0.18) if cuts else 1.0
    entries = jax.random.normal(stream_key, extent, jnp.float32) * deviation * level
    return jnp.minimum(jnp.maximum(entries, -bound), bound).astype(dtype)


def setup_inputs(seed: int = 0) -> dict:
    seeds = jax.random.split(jax.random.key(seed), 4)
    return {
        "sheet": draw_sheet(jax.random.fold_in(seeds[3], 71), 0),
        "w_in": gaussian(seeds[1], (D, HEADS, 6 * HDIM), D ** -0.5, 0.1875, ((1, 4),)),
        "w_out": gaussian(seeds[2], (HEADS, 2 * HDIM, D), (2 * D) ** -0.5, 0.125, ((0, 4),)),
    }


def head_norm(values):
    return values * lax.rsqrt(lax.optimization_barrier(jnp.mean(values * values, axis=-1, keepdims=True)) + 1e-06)

def feature_map(values):
    return jax.nn.elu(values) + 1.0

def finish_proj(proj):
    parts = [head_norm(proj[..., 0, :]), head_norm(proj[..., 1, :]), proj[..., 2, :], feature_map(proj[..., 3, :]), feature_map(proj[..., 4, :]), proj[..., 5, :]]
    return jnp.stack(parts, axis=-2).astype(jnp.bfloat16)

def reference(sheet, w_in, w_out):
    high = lax.Precision.HIGHEST
    xfull = sheet.astype(jnp.float32)
    normed = (xfull * lax.rsqrt(lax.optimization_barrier(jnp.mean(xfull * xfull, axis=-1, keepdims=True)) + 1e-06)).astype(jnp.bfloat16)
    flat = normed.reshape(COLS * ROWS, D)
    scale = HDIM ** (-0.5)
    blocks = ROWS // ROW_DEV
    causal = (jnp.arange(ROW_DEV)[:, None] >= jnp.arange(ROW_DEV)[None, :]).astype(jnp.float32)

    def one_head(total, inputs):
        w_head, w_back = inputs
        proj = jnp.dot(flat, w_head, preferred_element_type=jnp.float32).reshape(COLS, ROWS, 6, HDIM)
        parts = finish_proj(proj).astype(jnp.float32)
        qrow, krow, vrow = (parts[:, :, 0], parts[:, :, 1], parts[:, :, 2])
        fq, fk, vcol = (parts[:, :, 3], parts[:, :, 4], parts[:, :, 5])
        score = jnp.einsum('crd,erd->rce', qrow, krow) * scale
        expo = jnp.exp(score)
        weights = (expo / lax.optimization_barrier(jnp.sum(expo, axis=-1, keepdims=True))).astype(jnp.bfloat16)
        orow = jnp.einsum('rce,erd->crd', weights.astype(jnp.float32), vrow).astype(jnp.bfloat16)
        fqb = fq.reshape(COLS, blocks, ROW_DEV, HDIM)
        fkb = fk.reshape(COLS, blocks, ROW_DEV, HDIM)
        vcb = vcol.reshape(COLS, blocks, ROW_DEV, HDIM)
        states = jnp.einsum('cbsk,cbsv->cbkv', fkb, vcb, precision=high)
        running = jnp.cumsum(states, axis=1)
        prior = jnp.concatenate([jnp.zeros_like(running[:, :1]), running[:, :-1]], axis=1)
        carried = jnp.einsum('cbtk,cbkv->cbtv', fqb, prior, precision=high)
        inner = jnp.einsum('cbtd,cbsd->cbts', fqb, fkb, precision=high) * causal
        local = jnp.einsum('cbts,cbsv->cbtv', inner, vcb, precision=high)
        pre = (carried + local).reshape(COLS, ROWS, HDIM)
        ocol = head_norm(pre).astype(jnp.bfloat16)
        both = jnp.concatenate([orow, ocol], axis=-1).reshape(COLS * ROWS, 2 * HDIM)
        return (total + jnp.dot(both, w_back, preferred_element_type=jnp.float32), None)
    start = jnp.zeros((COLS * ROWS, D), jnp.float32)
    total, unused = lax.scan(one_head, start, (jnp.moveaxis(w_in, 1, 0), w_out))
    return total.reshape(COLS, ROWS, D).astype(jnp.bfloat16)
```

```python
import functools

import jax
import jax.numpy as jnp
from jax import lax
from jax.experimental import pallas as pl
from jax.experimental.pallas import tpu as pltpu
from jax.sharding import PartitionSpec as P

MESH = pl.DeviceIdType.MESH
F32, BF16 = jnp.float32, jnp.bfloat16
EPS = 1e-06
GROUP = 16


def dot(a, b, dims=((1,), (0,))):
    return lax.dot_general(a, b, (dims, ((), ())), preferred_element_type=F32)


def kernel(n, stages, x_ref, w_hbm, wo_hbm, out_ref, w, wo, buf, feat, tot, prior, st_send, st_recv, res, psend,
           precv, acc, load_sem, right_send, right_recv, left_send, left_recv, st_ssem, st_rsem, p_ssem, p_rsem):
    own, rows, width = x_ref.shape
    heads = w.shape[1] // 384
    hdim = 64
    c = lax.axis_index("cols")
    r = lax.axis_index("rows")

    w_copy = pltpu.make_async_copy(w_hbm, w, load_sem.at[0])
    wo_copy = pltpu.make_async_copy(wo_hbm, wo, load_sem.at[1])
    w_copy.start()
    wo_copy.start()

    both = jnp.minimum(c, n - 1 - c)
    more_left = c > n - 1 - c

    def place(s):
        paired = s <= 2 * both
        dist = jnp.where(paired, (s + 1) // 2, s - both)
        is_left = jnp.where(paired, s % 2 == 1, more_left)
        return dist, is_left, jnp.where(is_left, c - dist, c + dist)

    barrier = pltpu.get_barrier_semaphore()
    for s in range(1, n):
        pl.semaphore_signal(barrier, inc=1, device_id={"cols": lax.rem(c + s, n)}, device_id_type=MESH)
    for k in range(stages):
        pl.semaphore_signal(barrier, inc=1, device_id={"rows": partner(r, k)}, device_id_type=MESH)

    for i in range(own):
        xf = x_ref[i].astype(F32)
        buf[c, i] = (xf * lax.rsqrt(jnp.mean(xf * xf, axis=-1, keepdims=True) + EPS)).astype(BF16)
    pl.semaphore_wait(barrier, n - 1 + stages)

    def hop(shard, i, to_right):
        ssem, rsem = (right_send, right_recv) if to_right else (left_send, left_recv)
        to = jnp.minimum(c + 1, n - 1) if to_right else jnp.maximum(c - 1, 0)
        return pltpu.make_async_remote_copy(
            src_ref=buf.at[shard, i], dst_ref=buf.at[shard, i], send_sem=ssem.at[shard, i], recv_sem=rsem.at[shard, i],
            device_id={"cols": to}, device_id_type=MESH)

    for i in range(own):
        @pl.when(c < n - 1)
        def _():
            hop(c, i, True).start()

        @pl.when(c > 0)
        def _():
            hop(c, i, False).start()

    lane = lax.broadcasted_iota(jnp.int32, (1, 128), 1)
    low = lane < hdim
    spread = jnp.where(
        (lax.broadcasted_iota(jnp.int32, (128, 128), 0) < hdim) == (lax.broadcasted_iota(jnp.int32, (128, 128), 1) < hdim),
        1.0 / hdim, 0.0).astype(BF16)

    def phi(v):
        return jnp.where(v > 0, v + 1.0, jnp.exp(jnp.minimum(v, 0.0)))

    def project(s, shard):
        for i in range(own):
            xn = buf[shard, i]
            states = []
            for h in range(heads):
                proj = dot(xn, w[:, h * 384:(h + 1) * 384])
                t0, t1, t2 = proj[:, :128], proj[:, 128:256], proj[:, 256:]
                t0 = t0 * lax.rsqrt(dot((t0 * t0).astype(BF16), spread) + EPS)
                t1 = jnp.where(low, t1, phi(t1))
                t2 = jnp.where(low, phi(t2), t2).astype(BF16)
                feat[s, i, :, h * 384:h * 384 + 128] = t0.astype(BF16)
                feat[s, i, :, h * 384 + 128:h * 384 + 256] = t1.astype(BF16)
                feat[s, i, :, h * 384 + 256:h * 384 + 384] = t2
                states.append(dot(t2, t2, ((0,), (0,)))[:hdim, hdim:])
            tot[s, i] = jnp.concatenate(states, axis=-1)

    def exchange(s, k):
        return pltpu.make_async_remote_copy(
            src_ref=st_send.at[s, k], dst_ref=st_recv.at[s, k], send_sem=st_ssem.at[s, k], recv_sem=st_rsem.at[s, k],
            device_id={"rows": partner(r, k)}, device_id_type=MESH)

    def begin(s, k):
        st_send[s, k] = tot[s].astype(BF16)
        exchange(s, k).start()

    def advance(s, k):
        exchange(s, k).wait()
        got = st_recv[s, k].astype(F32)
        later = ((r // (1 << k)) % 2).astype(F32)
        prior[s] += got * later
        if k + 1 < stages:
            tot[s] += got
            begin(s, k + 1)

    prior[...] = jnp.zeros_like(prior)
    pending = []

    def tick():
        for at in list(pending):
            advance(*at)
            pending.remove(at)
            if at[1] + 1 < stages:
                pending.append((at[0], at[1] + 1))

    w_copy.wait()
    for s in range(n):
        dist, is_left, shard = place(s) if s else (0, None, c)
        if s:
            for i in range(own):
                @pl.when(is_left)
                def _():
                    hop(shard, i, True).wait_recv()

                    @pl.when(c < n - 1)
                    def _():
                        hop(shard, i, True).start()

                @pl.when(jnp.logical_not(is_left))
                def _():
                    hop(shard, i, False).wait_recv()

                    @pl.when(c > 0)
                    def _():
                        hop(shard, i, False).start()
        project(s, shard)
        begin(s, 0)
        tick()
        pending.append((s, 0))

    cells = n * own * GROUP
    same = (lax.broadcasted_iota(jnp.int32, (cells, cells), 0) % GROUP) == (
        lax.broadcasted_iota(jnp.int32, (cells, cells), 1) % GROUP)

    def row_group(g, carry):
        at = pl.ds(pl.multiple_of(g * GROUP, GROUP), GROUP)
        for h in range(heads):
            t0 = feat[:, :, at, h * 384:h * 384 + 128].reshape(cells, 128)
            v = feat[:, :, at, h * 384 + 128:h * 384 + 256].reshape(cells, 128)[:, :hdim]
            score = dot(t0[:, :hdim], t0[:, hdim:], ((1,), (1,))) * (hdim ** -0.5)
            expo = jnp.where(same, jnp.exp(score), 0.0)
            weights = (expo / jnp.sum(expo, axis=-1, keepdims=True)).astype(BF16)
            orow = dot(weights, v).astype(BF16)
            res[:, :, at, h * 128:h * 128 + hdim] = orow.reshape(n, own, GROUP, hdim)
        return carry

    groups = rows // GROUP
    cuts = [groups * p // stages for p in range(stages + 1)]
    for p in range(stages):
        lax.fori_loop(cuts[p], cuts[p + 1], row_group, 0)
        tick()
    while pending:
        tick()

    causal = lax.broadcasted_iota(jnp.int32, (rows, rows), 0) >= lax.broadcasted_iota(jnp.int32, (rows, rows), 1)

    def columns(s):
        for i in range(own):
            for h in range(heads):
                fq = feat[s, i, :, h * 384 + 128:h * 384 + 256][:, hdim:]
                t2 = feat[s, i, :, h * 384 + 256:h * 384 + 384]
                fk, vcol = t2[:, :hdim], t2[:, hdim:]
                inner = jnp.where(causal, dot(fq, fk, ((1,), (1,))), 0.0).astype(BF16)
                pre = dot(inner, vcol) + dot(fq, prior[s, i, :, h * hdim:(h + 1) * hdim].astype(BF16))
                ocol = pre * lax.rsqrt(jnp.mean(pre * pre, axis=-1, keepdims=True) + EPS)
                res[s, i, :, h * 128 + hdim:(h + 1) * 128] = ocol.astype(BF16)

    def partial(s, shard):
        return pltpu.make_async_remote_copy(
            src_ref=psend.at[s], dst_ref=precv.at[c], send_sem=p_ssem.at[s], recv_sem=p_rsem.at[c],
            device_id={"cols": shard}, device_id_type=MESH)

    wo_copy.wait()
    for s in list(range(n - 1, 0, -1)) + [0]:
        columns(s)
        for i in range(own):
            part = dot(res[s, i], wo[...])
            if s:
                psend[s, i] = part.astype(BF16)
            else:
                acc[i] = part
        if s:
            partial(s, place(s)[2]).start()

    for s in range(1, n):
        shard = place(s)[2]
        pltpu.make_async_remote_copy(
            src_ref=psend.at[s], dst_ref=precv.at[shard], send_sem=p_ssem.at[s], recv_sem=p_rsem.at[shard],
            device_id={"cols": shard}, device_id_type=MESH).wait_recv()
        for i in range(own):
            acc[i] += precv[shard, i].astype(F32)
    for i in range(own):
        out_ref[i] = acc[i].astype(BF16)

    for s in range(1, n):
        partial(s, place(s)[2]).wait_send()
    for shard in range(n):
        for i in range(own):
            @pl.when(jnp.logical_and(shard <= c, c < n - 1))
            def _():
                hop(shard, i, True).wait_send()

            @pl.when(jnp.logical_and(shard >= c, c > 0))
            def _():
                hop(shard, i, False).wait_send()


def partner(r, k):
    bit = (r // (1 << k)) % 2
    return r + (1 - 2 * bit) * (1 << k)


def body(n, nr, sheet, w_in, w_out):
    own, rows, width = sheet.shape
    heads = w_in.shape[1]
    hdim = w_out.shape[1] // 2
    stages = nr.bit_length() - 1
    vm = pltpu.VMEM
    dma = pltpu.SemaphoreType.DMA
    w_flat = w_in.reshape(width, heads * 6 * hdim)
    wo_flat = w_out.reshape(heads * 2 * hdim, width)
    return pl.pallas_call(
        functools.partial(kernel, n, stages),
        out_shape=jax.ShapeDtypeStruct((own, rows, width), BF16),
        in_specs=[pl.BlockSpec(memory_space=pltpu.VMEM), pl.BlockSpec(memory_space=pl.ANY),
                  pl.BlockSpec(memory_space=pl.ANY)],
        out_specs=pl.BlockSpec(memory_space=pltpu.VMEM),
        scratch_shapes=[
            vm(w_flat.shape, BF16),
            vm(wo_flat.shape, BF16),
            vm((n, own, rows, width), BF16),
            vm((n, own, rows, heads * 6 * hdim), BF16),
            vm((n, own, hdim, heads * hdim), F32),
            vm((n, own, hdim, heads * hdim), F32),
            vm((n, stages, own, hdim, heads * hdim), BF16),
            vm((n, stages, own, hdim, heads * hdim), BF16),
            vm((n, own, rows, heads * 2 * hdim), BF16),
            vm((n, own, rows, width), BF16),
            vm((n, own, rows, width), BF16),
            vm((own, rows, width), F32),
            dma((2,)), dma((n, own)), dma((n, own)), dma((n, own)), dma((n, own)),
            dma((n, stages)), dma((n, stages)), dma((n,)), dma((n,)),
        ],
        compiler_params=pltpu.CompilerParams(
            collective_id=0, has_side_effects=True, vmem_limit_bytes=56 * 1024 * 1024),
    )(sheet, w_flat, wo_flat)


def solution(mesh):
    return jax.shard_map(
        functools.partial(body, mesh.shape["cols"], mesh.shape["rows"]),
        mesh=mesh,
        in_specs=(P("cols", "rows", None), P(None, "cols", None), P("cols", None, None)),
        out_specs=P("cols", "rows", None),
        check_vma=False,
    )
```

```python
import functools

import jax
import jax.numpy as jnp
from jax import lax
from jax.experimental import pallas as pl
from jax.experimental.pallas import tpu as pltpu
from jax.sharding import PartitionSpec as P

MESH = pl.DeviceIdType.MESH
F32, BF16 = jnp.float32, jnp.bfloat16
EPS = 1e-06
GROUP = 16
PARTS = 2


def dot(a, b, dims=((1,), (0,))):
    return lax.dot_general(a, b, (dims, ((), ())), preferred_element_type=F32)


def kernel(n, stages, x_ref, w_hbm, wo_hbm, out_ref, w, w_all, buf, feat, tot, prior, st_send, st_recv, row_res,
           col_res, row_got, col_got, acc, load_sem, wo_sem, right_send, right_recv, left_send, left_recv, st_ssem,
           st_rsem, wz_ssem, wz_rsem, wb_ssem, wb_rsem, row_ssem, row_rsem, col_ssem, col_rsem):
    own, rows, width = x_ref.shape
    heads = w.shape[1] // 384
    hdim = 64
    c = lax.axis_index("cols")
    r = lax.axis_index("rows")

    w_copy = pltpu.make_async_copy(w_hbm, w, load_sem.at[0])
    w_copy.start()

    nr = w_all.shape[1]
    per = nr // (2 * heads)
    wo_copies = [
        pltpu.make_async_copy(
            wo_hbm.at[pl.ds((h * 2 + kind) * per, per)],
            w_all.at[c, pl.ds((kind * heads + h) * per, per)],
            wo_sem.at[kind, h])
        for kind in range(2) for h in range(heads)]
    for copy in wo_copies:
        copy.start()

    both = jnp.minimum(c, n - 1 - c)
    more_left = c > n - 1 - c

    def place(s):
        paired = s <= 2 * both
        dist = jnp.where(paired, (s + 1) // 2, s - both)
        is_left = jnp.where(paired, s % 2 == 1, more_left)
        return dist, is_left, jnp.where(is_left, c - dist, c + dist)

    barrier = pltpu.get_barrier_semaphore()
    for s in range(1, n):
        pl.semaphore_signal(barrier, inc=1, device_id={"cols": lax.rem(c + s, n)}, device_id_type=MESH)
    for t in range(1, nr):
        pl.semaphore_signal(barrier, inc=1, device_id={"rows": lax.rem(r + t, nr)}, device_id_type=MESH)

    for i in range(own):
        xf = x_ref[i].astype(F32)
        buf[c, i] = (xf * lax.rsqrt(jnp.mean(xf * xf, axis=-1, keepdims=True) + EPS)).astype(BF16)
    pl.semaphore_wait(barrier, n - 1 + nr - 1)

    def hop(shard, i, to_right):
        ssem, rsem = (right_send, right_recv) if to_right else (left_send, left_recv)
        to = jnp.minimum(c + 1, n - 1) if to_right else jnp.maximum(c - 1, 0)
        return pltpu.make_async_remote_copy(
            src_ref=buf.at[shard, i], dst_ref=buf.at[shard, i], send_sem=ssem.at[shard, i], recv_sem=rsem.at[shard, i],
            device_id={"cols": to}, device_id_type=MESH)

    for i in range(own):
        @pl.when(c < n - 1)
        def _():
            hop(c, i, True).start()

        @pl.when(c > 0)
        def _():
            hop(c, i, False).start()

    for copy in wo_copies:
        copy.wait()

    def give(s):
        return pltpu.make_async_remote_copy(
            src_ref=w_all.at[c, r], dst_ref=w_all.at[c, r], send_sem=wz_ssem.at[s], recv_sem=wz_rsem.at[c],
            device_id={"cols": lax.rem(c + s, n)}, device_id_type=MESH)

    def spread_out(j, t):
        return pltpu.make_async_remote_copy(
            src_ref=w_all.at[j, r], dst_ref=w_all.at[j, r], send_sem=wb_ssem.at[j, t], recv_sem=wb_rsem.at[j, r],
            device_id={"rows": lax.rem(r + t, nr)}, device_id_type=MESH)

    for s in range(1, n):
        give(s).start()

    def pass_on(j):
        pltpu.make_async_remote_copy(
            src_ref=w_all.at[j, r], dst_ref=w_all.at[j, r], send_sem=wz_ssem.at[0], recv_sem=wz_rsem.at[j],
            device_id={"cols": j}, device_id_type=MESH).wait_recv()
        for t in range(1, nr):
            spread_out(j, t).start()

    lane = lax.broadcasted_iota(jnp.int32, (1, 128), 1)
    low = lane < hdim
    spread = jnp.where(
        (lax.broadcasted_iota(jnp.int32, (128, 128), 0) < hdim) == (lax.broadcasted_iota(jnp.int32, (128, 128), 1) < hdim),
        1.0 / hdim, 0.0).astype(BF16)

    def phi(v):
        return jnp.where(v > 0, v + 1.0, jnp.exp(jnp.minimum(v, 0.0)))

    def project(s, shard, i):
        xn = buf[shard, i]
        states = []
        for h in range(heads):
            proj = dot(xn, w[:, h * 384:(h + 1) * 384])
            t0, t1, t2 = proj[:, :128], proj[:, 128:256], proj[:, 256:]
            t0 = t0 * lax.rsqrt(dot((t0 * t0).astype(BF16), spread) + EPS)
            t1 = jnp.where(low, t1, phi(t1))
            t2 = jnp.where(low, phi(t2), t2).astype(BF16)
            feat[s, i, :, h * 384:h * 384 + 128] = t0.astype(BF16)
            feat[s, i, :, h * 384 + 128:h * 384 + 256] = t1.astype(BF16)
            feat[s, i, :, h * 384 + 256:h * 384 + 384] = t2
            states.append(dot(t2, t2, ((0,), (0,)))[:hdim, hdim:])
        tot[s, i] = jnp.concatenate(states, axis=-1)

    def exchange(s, k):
        return pltpu.make_async_remote_copy(
            src_ref=st_send.at[s, k], dst_ref=st_recv.at[s, k], send_sem=st_ssem.at[s, k], recv_sem=st_rsem.at[s, k],
            device_id={"rows": partner(r, k)}, device_id_type=MESH)

    def begin(s, k):
        st_send[s, k] = tot[s].astype(BF16)
        exchange(s, k).start()

    def advance(s, k):
        exchange(s, k).wait()
        got = st_recv[s, k].astype(F32)
        later = ((r // (1 << k)) % 2).astype(F32)
        prior[s] += got * later
        if k + 1 < stages:
            tot[s] += got
            begin(s, k + 1)

    causal = lax.broadcasted_iota(jnp.int32, (rows, rows), 0) >= lax.broadcasted_iota(jnp.int32, (rows, rows), 1)

    def columns(s):
        for i in range(own):
            for h in range(heads):
                fq = feat[s, i, :, h * 384 + 128:h * 384 + 256][:, hdim:]
                t2 = feat[s, i, :, h * 384 + 256:h * 384 + 384]
                fk, vcol = t2[:, :hdim], t2[:, hdim:]
                inner = jnp.where(causal, dot(fq, fk, ((1,), (1,))), 0.0).astype(BF16)
                pre = dot(inner, vcol) + dot(fq, prior[s, i, :, h * hdim:(h + 1) * hdim].astype(BF16))
                ocol = pre * lax.rsqrt(jnp.mean(pre * pre, axis=-1, keepdims=True) + EPS)
                col_res[s, i, :, h * hdim:(h + 1) * hdim] = ocol.astype(BF16)

    def col_copy(s, slot):
        return pltpu.make_async_remote_copy(
            src_ref=col_res.at[s], dst_ref=col_got.at[slot], send_sem=col_ssem.at[s], recv_sem=col_rsem.at[slot],
            device_id={"cols": place(s)[2]}, device_id_type=MESH)

    def row_copy(s, p, slot):
        at = pl.ds(p * (rows // PARTS), rows // PARTS)
        return pltpu.make_async_remote_copy(
            src_ref=row_res.at[s, :, at], dst_ref=row_got.at[slot, :, at], send_sem=row_ssem.at[s, p],
            recv_sem=row_rsem.at[slot, p], device_id={"cols": place(s)[2]}, device_id_type=MESH)

    prior[...] = jnp.zeros_like(prior)
    pending = []

    def tick():
        for at in list(pending):
            advance(*at)
            pending.remove(at)
            if at[1] + 1 < stages:
                pending.append((at[0], at[1] + 1))
            else:
                columns(at[0])
                if at[0]:
                    col_copy(at[0], c).start()

    w_copy.wait()
    for s in range(n):
        dist, is_left, shard = place(s) if s else (0, None, c)
        for i in range(own):
            if s:
                @pl.when(is_left)
                def _():
                    hop(shard, i, True).wait_recv()

                    @pl.when(c < n - 1)
                    def _():
                        hop(shard, i, True).start()

                @pl.when(jnp.logical_not(is_left))
                def _():
                    hop(shard, i, False).wait_recv()

                    @pl.when(c > 0)
                    def _():
                        hop(shard, i, False).start()
            project(s, shard, i)
            if i == own - 1:
                begin(s, 0)
            tick()
        pending.append((s, 0))
        if s == 1:
            pass_on(place(1)[2])
        if s == 2:
            for later in range(2, n):
                pass_on(place(later)[2])

    cells = n * own * GROUP
    same = (lax.broadcasted_iota(jnp.int32, (cells, cells), 0) % GROUP) == (
        lax.broadcasted_iota(jnp.int32, (cells, cells), 1) % GROUP)

    def row_group(g, carry):
        at = pl.ds(pl.multiple_of(g * GROUP, GROUP), GROUP)
        for h in range(heads):
            t0 = feat[:, :, at, h * 384:h * 384 + 128].reshape(cells, 128)
            v = feat[:, :, at, h * 384 + 128:h * 384 + 256].reshape(cells, 128)[:, :hdim]
            score = dot(t0[:, :hdim], t0[:, hdim:], ((1,), (1,))) * (hdim ** -0.5)
            expo = jnp.where(same, jnp.exp(score), 0.0)
            weights = (expo / jnp.sum(expo, axis=-1, keepdims=True)).astype(BF16)
            orow = dot(weights, v).astype(BF16)
            row_res[:, :, at, h * hdim:(h + 1) * hdim] = orow.reshape(n, own, GROUP, hdim)
        return carry

    groups = rows // GROUP
    for p in range(PARTS):
        lax.fori_loop(groups * p // PARTS, groups * (p + 1) // PARTS, row_group, 0)
        for s in range(n - 1, 0, -1):
            row_copy(s, p, c).start()
        tick()
    while pending:
        tick()

    def combine(slot, i, row, col):
        half = nr // 2
        w_row = w_all[slot, :half].reshape(heads * hdim, width)
        w_col = w_all[slot, half:].reshape(heads * hdim, width)
        return dot(row, w_row) + dot(col, w_col)

    for i in range(own):
        acc[i] = combine(c, i, row_res[0, i], col_res[0, i])
    for s in range(1, n):
        shard = place(s)[2]
        for t in range(1, nr):
            sender = lax.rem(r + t, nr)
            pltpu.make_async_remote_copy(
                src_ref=w_all.at[shard, sender], dst_ref=w_all.at[shard, sender], send_sem=wb_ssem.at[shard, t],
                recv_sem=wb_rsem.at[shard, sender], device_id={"rows": sender}, device_id_type=MESH).wait_recv()
        for p in range(PARTS):
            row_copy(s, p, shard).wait_recv()
        col_copy(s, shard).wait_recv()
        for i in range(own):
            acc[i] += combine(shard, i, row_got[shard, i], col_got[shard, i])
    for i in range(own):
        out_ref[i] = acc[i].astype(BF16)

    for s in range(1, n):
        give(s).wait_send()
        col_copy(s, c).wait_send()
        for p in range(PARTS):
            row_copy(s, p, c).wait_send()
        for t in range(1, nr):
            spread_out(place(s)[2], t).wait_send()
    for shard in range(n):
        for i in range(own):
            @pl.when(jnp.logical_and(shard <= c, c < n - 1))
            def _():
                hop(shard, i, True).wait_send()

            @pl.when(jnp.logical_and(shard >= c, c > 0))
            def _():
                hop(shard, i, False).wait_send()


def partner(r, k):
    bit = (r // (1 << k)) % 2
    return r + (1 - 2 * bit) * (1 << k)


def body(n, nr, sheet, w_in, w_out):
    own, rows, width = sheet.shape
    heads = w_in.shape[1]
    hdim = w_out.shape[1] // 2
    stages = nr.bit_length() - 1
    vm = pltpu.VMEM
    dma = pltpu.SemaphoreType.DMA
    w_flat = w_in.reshape(width, heads * 6 * hdim)
    wo_flat = w_out.reshape(nr, heads * 2 * hdim // nr, width)
    return pl.pallas_call(
        functools.partial(kernel, n, stages),
        out_shape=jax.ShapeDtypeStruct((own, rows, width), BF16),
        in_specs=[pl.BlockSpec(memory_space=pltpu.VMEM), pl.BlockSpec(memory_space=pl.ANY),
                  pl.BlockSpec(memory_space=pl.ANY)],
        out_specs=pl.BlockSpec(memory_space=pltpu.VMEM),
        scratch_shapes=[
            vm(w_flat.shape, BF16),
            vm((n,) + wo_flat.shape, BF16),
            vm((n, own, rows, width), BF16),
            vm((n, own, rows, heads * 6 * hdim), BF16),
            vm((n, own, hdim, heads * hdim), F32),
            vm((n, own, hdim, heads * hdim), F32),
            vm((n, stages, own, hdim, heads * hdim), BF16),
            vm((n, stages, own, hdim, heads * hdim), BF16),
            vm((n, own, rows, heads * hdim), BF16),
            vm((n, own, rows, heads * hdim), BF16),
            vm((n, own, rows, heads * hdim), BF16),
            vm((n, own, rows, heads * hdim), BF16),
            vm((own, rows, width), F32),
            dma((1,)), dma((2, heads)), dma((n, own)), dma((n, own)), dma((n, own)), dma((n, own)),
            dma((n, stages)), dma((n, stages)), dma((n,)), dma((n,)), dma((n, nr)), dma((n, nr)),
            dma((n, PARTS)), dma((n, PARTS)), dma((n,)), dma((n,)),
        ],
        compiler_params=pltpu.CompilerParams(
            collective_id=0, has_side_effects=True, vmem_limit_bytes=56 * 1024 * 1024),
    )(sheet, w_flat, wo_flat)


def solution(mesh):
    return jax.shard_map(
        functools.partial(body, mesh.shape["cols"], mesh.shape["rows"]),
        mesh=mesh,
        in_specs=(P("cols", "rows", None), P(None, "cols", None), P("cols", None, None)),
        out_specs=P("cols", "rows", None),
        check_vma=False,
    )
```

```python
import functools

import jax
import jax.numpy as jnp
from jax import lax
from jax.experimental import pallas as pl
from jax.experimental.pallas import tpu as pltpu
from jax.sharding import PartitionSpec as P

MESH = pl.DeviceIdType.MESH
F32, BF16 = jnp.float32, jnp.bfloat16
EPS = 1e-06
GROUP = 16
PARTS = 2


def dot(a, b, dims=((1,), (0,))):
    return lax.dot_general(a, b, (dims, ((), ())), preferred_element_type=F32)


def kernel(n, stages, x_ref, w_hbm, wo_hbm, out_ref, w, w_all, buf, feat, tot, prior, st_send, st_recv, row_res,
           col_res, row_got, col_got, acc, load_sem, wo_sem, right_send, right_recv, left_send, left_recv, st_ssem,
           st_rsem, wz_ssem, wz_rsem, wb_ssem, wb_rsem, row_ssem, row_rsem, col_ssem, col_rsem):
    own, rows, width = x_ref.shape
    heads = w.shape[1] // 384
    hdim = 64
    c = lax.axis_index("cols")
    r = lax.axis_index("rows")

    w_copy = pltpu.make_async_copy(w_hbm, w, load_sem.at[0])
    w_copy.start()

    nr = w_all.shape[1]
    per = nr // (2 * heads)
    wo_copies = [
        pltpu.make_async_copy(
            wo_hbm.at[pl.ds((h * 2 + kind) * per, per)],
            w_all.at[c, pl.ds((kind * heads + h) * per, per)],
            wo_sem.at[kind, h])
        for kind in range(2) for h in range(heads)]
    for copy in wo_copies:
        copy.start()

    both = jnp.minimum(c, n - 1 - c)
    more_left = c > n - 1 - c

    def place(s):
        paired = s <= 2 * both
        dist = jnp.where(paired, (s + 1) // 2, s - both)
        is_left = jnp.where(paired, s % 2 == 1, more_left)
        return dist, is_left, jnp.where(is_left, c - dist, c + dist)

    barrier = pltpu.get_barrier_semaphore()
    for s in range(1, n):
        pl.semaphore_signal(barrier, inc=1, device_id={"cols": lax.rem(c + s, n)}, device_id_type=MESH)
    for t in range(1, nr):
        pl.semaphore_signal(barrier, inc=1, device_id={"rows": lax.rem(r + t, nr)}, device_id_type=MESH)

    for i in range(own):
        xf = x_ref[i].astype(F32)
        buf[c, i] = (xf * lax.rsqrt(jnp.mean(xf * xf, axis=-1, keepdims=True) + EPS)).astype(BF16)
    pl.semaphore_wait(barrier, n - 1 + nr - 1)

    def hop(shard, i, to_right):
        ssem, rsem = (right_send, right_recv) if to_right else (left_send, left_recv)
        to = jnp.minimum(c + 1, n - 1) if to_right else jnp.maximum(c - 1, 0)
        return pltpu.make_async_remote_copy(
            src_ref=buf.at[shard, i], dst_ref=buf.at[shard, i], send_sem=ssem.at[shard, i], recv_sem=rsem.at[shard, i],
            device_id={"cols": to}, device_id_type=MESH)

    for i in range(own):
        @pl.when(c < n - 1)
        def _():
            hop(c, i, True).start()

        @pl.when(c > 0)
        def _():
            hop(c, i, False).start()

    for copy in wo_copies:
        copy.wait()

    def give(s):
        return pltpu.make_async_remote_copy(
            src_ref=w_all.at[c, r], dst_ref=w_all.at[c, r], send_sem=wz_ssem.at[s], recv_sem=wz_rsem.at[c],
            device_id={"cols": lax.rem(c + s, n)}, device_id_type=MESH)

    def spread_out(j, t):
        return pltpu.make_async_remote_copy(
            src_ref=w_all.at[j, r], dst_ref=w_all.at[j, r], send_sem=wb_ssem.at[j, t], recv_sem=wb_rsem.at[j, r],
            device_id={"rows": lax.rem(r + t, nr)}, device_id_type=MESH)

    for s in range(1, n):
        give(s).start()

    def pass_on(j):
        pltpu.make_async_remote_copy(
            src_ref=w_all.at[j, r], dst_ref=w_all.at[j, r], send_sem=wz_ssem.at[0], recv_sem=wz_rsem.at[j],
            device_id={"cols": j}, device_id_type=MESH).wait_recv()
        for t in range(1, nr):
            spread_out(j, t).start()

    lane = lax.broadcasted_iota(jnp.int32, (1, 128), 1)
    low = lane < hdim
    spread = jnp.where(
        (lax.broadcasted_iota(jnp.int32, (128, 128), 0) < hdim) == (lax.broadcasted_iota(jnp.int32, (128, 128), 1) < hdim),
        1.0 / hdim, 0.0).astype(BF16)

    def phi(v):
        return jnp.where(v > 0, v + 1.0, jnp.exp(jnp.minimum(v, 0.0)))

    def project(s, shard, i):
        xn = buf[shard, i]
        states = []
        for h in range(heads):
            proj = dot(xn, w[:, h * 384:(h + 1) * 384])
            t0, t1, t2 = proj[:, :128], proj[:, 128:256], proj[:, 256:]
            t0 = t0 * lax.rsqrt(dot((t0 * t0).astype(BF16), spread) + EPS)
            t1 = jnp.where(low, t1, phi(t1))
            t2 = jnp.where(low, phi(t2), t2).astype(BF16)
            feat[s, i, :, h * 384:h * 384 + 128] = t0.astype(BF16)
            feat[s, i, :, h * 384 + 128:h * 384 + 256] = t1.astype(BF16)
            feat[s, i, :, h * 384 + 256:h * 384 + 384] = t2
            states.append(dot(t2, t2, ((0,), (0,)))[:hdim, hdim:])
        tot[s, i] = jnp.concatenate(states, axis=-1)

    def exchange(s, k):
        return pltpu.make_async_remote_copy(
            src_ref=st_send.at[s, k], dst_ref=st_recv.at[s, k], send_sem=st_ssem.at[s, k], recv_sem=st_rsem.at[s, k],
            device_id={"rows": partner(r, k)}, device_id_type=MESH)

    def begin(s, k):
        st_send[s, k] = tot[s].astype(BF16)
        exchange(s, k).start()

    def advance(s, k):
        exchange(s, k).wait()
        got = st_recv[s, k].astype(F32)
        later = ((r // (1 << k)) % 2).astype(F32)
        prior[s] += got * later
        if k + 1 < stages:
            tot[s] += got
            begin(s, k + 1)

    causal = lax.broadcasted_iota(jnp.int32, (rows, rows), 0) >= lax.broadcasted_iota(jnp.int32, (rows, rows), 1)

    def columns(s):
        for i in range(own):
            for h in range(heads):
                fq = feat[s, i, :, h * 384 + 128:h * 384 + 256][:, hdim:]
                t2 = feat[s, i, :, h * 384 + 256:h * 384 + 384]
                fk, vcol = t2[:, :hdim], t2[:, hdim:]
                inner = jnp.where(causal, dot(fq, fk, ((1,), (1,))), 0.0).astype(BF16)
                pre = dot(inner, vcol) + dot(fq, prior[s, i, :, h * hdim:(h + 1) * hdim].astype(BF16))
                ocol = pre * lax.rsqrt(jnp.mean(pre * pre, axis=-1, keepdims=True) + EPS)
                col_res[s, i, :, h * hdim:(h + 1) * hdim] = ocol.astype(BF16)

    def col_copy(s, slot):
        return pltpu.make_async_remote_copy(
            src_ref=col_res.at[s], dst_ref=col_got.at[slot], send_sem=col_ssem.at[s], recv_sem=col_rsem.at[slot],
            device_id={"cols": place(s)[2]}, device_id_type=MESH)

    def row_copy(s, p, slot):
        at = pl.ds(p * (rows // PARTS), rows // PARTS)
        return pltpu.make_async_remote_copy(
            src_ref=row_res.at[s, :, at], dst_ref=row_got.at[slot, :, at], send_sem=row_ssem.at[s, p],
            recv_sem=row_rsem.at[slot, p], device_id={"cols": place(s)[2]}, device_id_type=MESH)

    prior[...] = jnp.zeros_like(prior)
    pending = []

    def tick():
        for at in list(pending):
            advance(*at)
            pending.remove(at)
            if at[1] + 1 < stages:
                pending.append((at[0], at[1] + 1))
            else:
                columns(at[0])
                if at[0]:
                    col_copy(at[0], c).start()

    w_copy.wait()
    for s in range(n):
        dist, is_left, shard = place(s) if s else (0, None, c)
        for i in range(own):
            if s:
                @pl.when(is_left)
                def _():
                    hop(shard, i, True).wait_recv()

                    @pl.when(c < n - 1)
                    def _():
                        hop(shard, i, True).start()

                @pl.when(jnp.logical_not(is_left))
                def _():
                    hop(shard, i, False).wait_recv()

                    @pl.when(c > 0)
                    def _():
                        hop(shard, i, False).start()
            project(s, shard, i)
            if i == own - 1:
                begin(s, 0)
            tick()
        pending.append((s, 0))
        if s == 1:
            pass_on(place(1)[2])
        if s == 2:
            for later in range(2, n):
                pass_on(place(later)[2])

    cells = n * own * GROUP
    same = (lax.broadcasted_iota(jnp.int32, (cells, cells), 0) % GROUP) == (
        lax.broadcasted_iota(jnp.int32, (cells, cells), 1) % GROUP)

    def row_group(g, carry):
        at = pl.ds(pl.multiple_of(g * GROUP, GROUP), GROUP)
        for h in range(heads):
            t0 = feat[:, :, at, h * 384:h * 384 + 128].reshape(cells, 128)
            v = feat[:, :, at, h * 384 + 128:h * 384 + 256].reshape(cells, 128)
            score = dot(t0[:, :hdim], t0[:, hdim:], ((1,), (1,))) * (hdim ** -0.5)
            expo = jnp.where(same, jnp.exp(score), 0.0).astype(BF16)
            both_sums = dot(expo, jnp.where(low, v, jnp.ones_like(v)))
            orow = (both_sums[:, :hdim] / both_sums[:, hdim:]).astype(BF16)
            row_res[:, :, at, h * hdim:(h + 1) * hdim] = orow.reshape(n, own, GROUP, hdim)
        return carry

    groups = rows // GROUP
    for p in range(PARTS):
        lax.fori_loop(groups * p // PARTS, groups * (p + 1) // PARTS, row_group, 0)
        for s in range(n - 1, 0, -1):
            row_copy(s, p, c).start()
        tick()
    while pending:
        tick()

    def combine(slot, i, row, col):
        half = nr // 2
        w_row = w_all[slot, :half].reshape(heads * hdim, width)
        w_col = w_all[slot, half:].reshape(heads * hdim, width)
        return dot(row, w_row) + dot(col, w_col)

    for i in range(own):
        acc[i] = combine(c, i, row_res[0, i], col_res[0, i])
    for s in range(1, n):
        shard = place(s)[2]
        for t in range(1, nr):
            sender = lax.rem(r + t, nr)
            pltpu.make_async_remote_copy(
                src_ref=w_all.at[shard, sender], dst_ref=w_all.at[shard, sender], send_sem=wb_ssem.at[shard, t],
                recv_sem=wb_rsem.at[shard, sender], device_id={"rows": sender}, device_id_type=MESH).wait_recv()
        for p in range(PARTS):
            row_copy(s, p, shard).wait_recv()
        col_copy(s, shard).wait_recv()
        for i in range(own):
            acc[i] += combine(shard, i, row_got[shard, i], col_got[shard, i])
    for i in range(own):
        out_ref[i] = acc[i].astype(BF16)

    for s in range(1, n):
        give(s).wait_send()
        col_copy(s, c).wait_send()
        for p in range(PARTS):
            row_copy(s, p, c).wait_send()
        for t in range(1, nr):
            spread_out(place(s)[2], t).wait_send()
    for shard in range(n):
        for i in range(own):
            @pl.when(jnp.logical_and(shard <= c, c < n - 1))
            def _():
                hop(shard, i, True).wait_send()

            @pl.when(jnp.logical_and(shard >= c, c > 0))
            def _():
                hop(shard, i, False).wait_send()


def partner(r, k):
    bit = (r // (1 << k)) % 2
    return r + (1 - 2 * bit) * (1 << k)


def body(n, nr, sheet, w_in, w_out):
    own, rows, width = sheet.shape
    heads = w_in.shape[1]
    hdim = w_out.shape[1] // 2
    stages = nr.bit_length() - 1
    vm = pltpu.VMEM
    dma = pltpu.SemaphoreType.DMA
    w_flat = w_in.reshape(width, heads * 6 * hdim)
    wo_flat = w_out.reshape(nr, heads * 2 * hdim // nr, width)
    return pl.pallas_call(
        functools.partial(kernel, n, stages),
        out_shape=jax.ShapeDtypeStruct((own, rows, width), BF16),
        in_specs=[pl.BlockSpec(memory_space=pltpu.VMEM), pl.BlockSpec(memory_space=pl.ANY),
                  pl.BlockSpec(memory_space=pl.ANY)],
        out_specs=pl.BlockSpec(memory_space=pltpu.VMEM),
        scratch_shapes=[
            vm(w_flat.shape, BF16),
            vm((n,) + wo_flat.shape, BF16),
            vm((n, own, rows, width), BF16),
            vm((n, own, rows, heads * 6 * hdim), BF16),
            vm((n, own, hdim, heads * hdim), F32),
            vm((n, own, hdim, heads * hdim), F32),
            vm((n, stages, own, hdim, heads * hdim), BF16),
            vm((n, stages, own, hdim, heads * hdim), BF16),
            vm((n, own, rows, heads * hdim), BF16),
            vm((n, own, rows, heads * hdim), BF16),
            vm((n, own, rows, heads * hdim), BF16),
            vm((n, own, rows, heads * hdim), BF16),
            vm((own, rows, width), F32),
            dma((1,)), dma((2, heads)), dma((n, own)), dma((n, own)), dma((n, own)), dma((n, own)),
            dma((n, stages)), dma((n, stages)), dma((n,)), dma((n,)), dma((n, nr)), dma((n, nr)),
            dma((n, PARTS)), dma((n, PARTS)), dma((n,)), dma((n,)),
        ],
        compiler_params=pltpu.CompilerParams(
            collective_id=0, has_side_effects=True, vmem_limit_bytes=56 * 1024 * 1024),
    )(sheet, w_flat, wo_flat)


def solution(mesh):
    return jax.shard_map(
        functools.partial(body, mesh.shape["cols"], mesh.shape["rows"]),
        mesh=mesh,
        in_specs=(P("cols", "rows", None), P(None, "cols", None), P("cols", None, None)),
        out_specs=P("cols", "rows", None),
        check_vma=False,
    )
```
